32 devices in a mesh: gx: 4 (over x, core), gy: 4 (over z), gz: 2 (over y).
Axes of the slice: x: 2, y: 2, z: 4, core: 2. Of those that a mesh axis runs over, the one named last changes fastest.
Arguments:
- load_data: float32 [4, 4, 2, 128, 1536], P('gx', 'gy', 'gz'), may hold values from -6 to 6
- initial_dual: float32 [4, 4, 2, 128, 1536], P('gx', 'gy', 'gz'), may hold values from -6 to 6
- dual_operator: float32 [4, 4, 2, 1536, 1536], P('gx', 'gy', 'gz'), as said below
- coarse_modes: float32 [4, 4, 2, 64, 1536], P('gx', 'gy', 'gz'), may hold values from -0.15625 to 0.15625
- coarse_inverse: float32 [2048, 2048], P(('gx', 'gy', 'gz')), as said below
- face_start: int32 [4, 4, 2, 6], P('gx', 'gy', 'gz'), may hold values from 0 to 1535, as said below
- face_len: int32 [4, 4, 2, 6], P('gx', 'gy', 'gz'), may hold values from 128 to 256, as said below
- multiplicity: int32 [4, 4, 2, 1536], P('gx', 'gy', 'gz'), may hold values from 2 to 4
Outputs:
- dual_solution: float32 [4, 4, 2, 128, 1536], P('gx', 'gy', 'gz')
- final_residual: float32 [4, 4, 2, 128, 1536], P('gx', 'gy', 'gz')
The draws below stay inside these ranges and needn't reach their ends.
Inputs may be any that keep to these rules, and one draw needn't show every extreme that they name: `face_len`: on each subdomain the six face segments lie within 0 to 1535 and do not intersect; the pieces on the two faces that meet between neighbouring subdomains have the same length; some face between two subdomains has exactly 256 unknowns. `face_start`: start of each face segment; see face_len. `dual_operator`: each subdomain's block is symmetric. `coarse_inverse`: the matrix is symmetric.
All inputs are finite; a program needn't handle non-finite values.
Results may differ from the reference program's by a relative error of at most 0.0003.
Values sent between devices are 32-bit elements; how exact they have to be, the bound alone decides.
A program may use at most 128 MiB of HBM per device.

```python
import jax
import jax.numpy as jnp
from jax import lax

M = 1536
PCAP = 256
NM = 64
LOADS = 128
OUTER = 2
CHEB = 3
SX = 4
SY = 4
SZ = 2
C = 2048


def face_layout(key):
    base = jax.random.fold_in(key, 7001)
    keys = jax.random.split(base, 6)
    lowest = PCAP // 2
    len_x = jax.random.randint(keys[0], (SX + 1, SY, SZ), lowest, PCAP + 1)
    len_y = jax.random.randint(keys[1], (SX, SY + 1, SZ), lowest, PCAP + 1)
    len_z = jax.random.randint(keys[2], (SX, SY, SZ + 1), lowest, PCAP + 1)
    chosen = jax.random.randint(keys[3], (), 0, (SX - 1) * SY * SZ) + SY * SZ
    len_x = len_x.reshape(-1).at[chosen].set(PCAP).reshape(SX + 1, SY, SZ)
    lengths = jnp.stack([len_x[:-1], len_x[1:], len_y[:, :-1], len_y[:, 1:], len_z[:, :, :-1], len_z[:, :, 1:]], axis=-1)
    scores = jax.random.randint(keys[4], (SX, SY, SZ, 6), 0, 1000) * 8 + jnp.arange(6, dtype=jnp.int32)
    placing = jnp.argsort(scores, axis=-1)
    ordered = jnp.take_along_axis(lengths, placing, axis=-1)
    slack = M - jnp.sum(lengths, axis=-1, keepdims=True)
    shares = jax.random.randint(keys[5], (SX, SY, SZ, 6), 1, 100)
    gaps = slack * shares // jnp.sum(shares, axis=-1, keepdims=True)
    starts_ordered = jnp.cumsum(gaps + ordered, axis=-1) - ordered
    inverse = jnp.argsort(placing, axis=-1)
    starts = jnp.take_along_axis(starts_ordered, inverse, axis=-1)
    return (starts.astype(jnp.int32), lengths.astype(jnp.int32))


def draw_face_start(key, part):
    return face_layout(key)[0]


def draw_face_len(key, part):
    return face_layout(key)[1]


def symmetric_matrix(key, leading, order, spread):
    keys = jax.random.split(jax.random.fold_in(key, 7002), 2)
    shape = leading + (order, order)
    diagonal = jnp.exp(jax.random.uniform(keys[0], leading + (order,), jnp.float32, jnp.log(0.5), jnp.log(1.5)))
    coupling = jax.random.normal(keys[1], shape, jnp.float32)
    coupling = (coupling + jnp.swapaxes(coupling, -1, -2)) * (spread / jnp.sqrt(2.0 * order))
    identity = jnp.eye(order, dtype=jnp.float32)
    return coupling + diagonal[..., None] * identity


def draw_dual_operator(key, part):
    return symmetric_matrix(key, (SX, SY, SZ), M, 0.25)


def draw_coarse_inverse(key, part):
    return symmetric_matrix(key, (), C, 0.3)


def place_ends(entries, stream_key, smallest, top_value):
    dims = entries.shape
    index_at = [jax.random.randint(jax.random.fold_in(stream_key, axis), (), 0, dims[axis]) for axis in range(len(dims))]
    entries = entries.at[tuple(index_at)].set(smallest)
    longest = dims.index(max(dims))
    index_at[longest] = (index_at[longest] + 1) % dims[longest]
    return entries.at[tuple(index_at)].set(top_value)


def block_scale(stream_key, shape, cuts, low, high):
    def one(position, blocks):
        draws = jax.random.uniform(jax.random.fold_in(jax.random.fold_in(stream_key, 6), position), (blocks,), jnp.float32, low / len(cuts), high / len(cuts))
        return jnp.repeat(jnp.exp(draws), shape[position] // blocks).reshape((-1,) + (1,) * (len(shape) - position - 1))

    gain = one(*cuts[0])
    for cut in cuts[1:]:
        gain = gain * one(*cut)
    return gain


def noise(stream_key, shape, scale, limit, shards=(), held_as=jnp.bfloat16):
    loudness = block_scale(stream_key, shape, shards, -0.22, 0.18) if shards else 1.0
    drawn = jax.random.normal(stream_key, shape, jnp.float32) * scale * loudness
    return jnp.minimum(jnp.maximum(drawn, -limit), limit).astype(held_as)


def setup_inputs(seed: int = 0) -> dict:
    key_list = jax.random.split(jax.random.key(seed), 9)
    load_data = noise(key_list[0], (SX, SY, SZ, LOADS, M), 1.0, 6.0, ((0, 4), (1, 4), (2, 2)), jnp.float32)
    initial_dual = noise(key_list[1], (SX, SY, SZ, LOADS, M), 1.0, 6.0, ((0, 4), (1, 4), (2, 2)), jnp.float32)
    dual_operator = draw_dual_operator(jax.random.fold_in(key_list[8], 71), 0)
    coarse_modes = noise(key_list[3], (SX, SY, SZ, NM, M), M ** -0.5, 0.15625, ((0, 4), (1, 4), (2, 2)), jnp.float32)
    coarse_inverse = draw_coarse_inverse(jax.random.fold_in(key_list[8], 71), 0)
    face_start = draw_face_start(jax.random.fold_in(key_list[8], 71), 0)
    face_len = draw_face_len(jax.random.fold_in(key_list[8], 71), 0)
    multiplicity = place_ends(jax.random.randint(key_list[7], (SX, SY, SZ, M), 2, 5), jax.random.fold_in(key_list[7], 1), 2, 4).astype(jnp.int32)
    return {"load_data": load_data, "initial_dual": initial_dual, "dual_operator": dual_operator, "coarse_modes": coarse_modes, "coarse_inverse": coarse_inverse, "face_start": face_start, "face_len": face_len, "multiplicity": multiplicity}


highest = lax.Precision.HIGHEST
center = 1.0
half_width = 0.9


def face_pieces(values, starts, lengths):
    padded = jnp.pad(values, ((0, 0), (0, PCAP)))
    offsets = jnp.arange(PCAP, dtype=jnp.int32)
    gathered = []
    for face_id in range(6):
        anchor = starts[face_id].astype(jnp.int32)
        segment = lax.dynamic_slice(padded, (jnp.int32(0), anchor), (values.shape[0], PCAP))
        gathered.append(jnp.where(offsets < lengths[face_id], segment, 0.0))
    return jnp.stack(gathered)


def place_pieces(values, received, starts, lengths):
    padded = jnp.pad(values, ((0, 0), (0, PCAP)))
    offsets = jnp.arange(PCAP, dtype=jnp.int32)
    for face_id in range(6):
        anchor = starts[face_id].astype(jnp.int32)
        window = lax.dynamic_slice(padded, (jnp.int32(0), anchor), (values.shape[0], PCAP))
        window = window + jnp.where(offsets < lengths[face_id], received[face_id], 0.0)
        padded = lax.dynamic_update_slice(padded, window, (jnp.int32(0), anchor))
    return padded[:, :values.shape[1]]


def from_lower(stacked, along):
    zeros_slab = jnp.zeros_like(lax.slice_in_dim(stacked, 0, 1, axis=along))
    return jnp.concatenate([zeros_slab, lax.slice_in_dim(stacked, 0, stacked.shape[along] - 1, axis=along)], along)


def from_upper(stacked, along):
    zeros_slab = jnp.zeros_like(lax.slice_in_dim(stacked, 0, 1, axis=along))
    return jnp.concatenate([lax.slice_in_dim(stacked, 1, stacked.shape[along], axis=along), zeros_slab], along)


def operate(vectors, operator, starts, lengths, inverse_weight):
    subdomains = SX * SY * SZ
    product = jnp.einsum('abckm,abcmn->abckn', vectors, operator, precision=highest)
    flat_product = product.reshape(subdomains, LOADS, M)
    flat_starts = starts.reshape(subdomains, 6)
    flat_lengths = lengths.reshape(subdomains, 6)
    pieces = jax.vmap(face_pieces)(flat_product, flat_starts, flat_lengths)
    pieces = pieces.reshape(SX, SY, SZ, 6, LOADS, PCAP)
    received = jnp.stack([
        from_lower(pieces[:, :, :, 1], 0), from_upper(pieces[:, :, :, 0], 0),
        from_lower(pieces[:, :, :, 3], 1), from_upper(pieces[:, :, :, 2], 1),
        from_lower(pieces[:, :, :, 5], 2), from_upper(pieces[:, :, :, 4], 2)], axis=3)
    received = received.reshape(subdomains, 6, LOADS, PCAP)
    summed = jax.vmap(place_pieces)(flat_product, received, flat_starts, flat_lengths)
    return summed.reshape(SX, SY, SZ, LOADS, M) * inverse_weight[:, :, :, None, :]


def project(vectors, coarse_modes, coarse_inverse):
    subdomains = SX * SY * SZ
    coeffs = jnp.einsum('abckm,abcjm->abckj', vectors, coarse_modes, precision=highest)
    coeff_all = coeffs.reshape(subdomains, LOADS, NM).transpose(1, 0, 2).reshape(LOADS, C)
    amplitude_all = lax.dot_general(coeff_all, coarse_inverse, (((1,), (1,)), ((), ())), precision=highest)
    amplitude = amplitude_all.reshape(LOADS, subdomains, NM).transpose(1, 0, 2).reshape(SX, SY, SZ, LOADS, NM)
    return vectors - jnp.einsum('abckj,abcjm->abckm', amplitude, coarse_modes, precision=highest)


def reference(load_data, initial_dual, dual_operator, coarse_modes, coarse_inverse, face_start, face_len, multiplicity):
    inverse_weight = 1.0 / multiplicity.astype(jnp.float32)
    multipliers = initial_dual
    for outer_idx in range(OUTER):
        residual = load_data - operate(multipliers, dual_operator, face_start, face_len, inverse_weight)
        stretch = center / half_width
        rho_now = 1.0 / stretch
        correction = residual / center
        for inner_idx in range(CHEB):
            multipliers = multipliers + correction
            if inner_idx < CHEB - 1:
                residual = residual - operate(correction, dual_operator, face_start, face_len, inverse_weight)
                rho_next = 1.0 / (2.0 * stretch - rho_now)
                correction = (rho_next * rho_now) * correction + (2.0 * rho_next / half_width) * residual
                rho_now = rho_next
        multipliers = project(multipliers, coarse_modes, coarse_inverse)
    final_residual = load_data - operate(multipliers, dual_operator, face_start, face_len, inverse_weight)
    return multipliers, final_residual
```

```python
import functools

import jax
import jax.numpy as jnp
from jax import lax
from jax.experimental import pallas as pl
from jax.experimental.pallas import tpu as pltpu
from jax.sharding import PartitionSpec as P

PCAP = 256
OUTER = 2
CHEB = 3
TILE = 128
SLOT = PCAP + TILE
CHUNK = 768

CENTER = 1.0
HALF_WIDTH = 0.9

F32 = jnp.float32
BF16 = jnp.bfloat16
MESH = pl.DeviceIdType.MESH
AXES = ("gx", "gy", "gz")


def split(x):
    high = x.astype(BF16)
    return high, (x - high.astype(F32)).astype(BF16)


def dot(a, b):
    return jnp.dot(a, b, preferred_element_type=F32)


def triple(a_high, a_low, cat_ref):
    width = cat_ref.shape[1] // 2
    both = dot(a_high, cat_ref[...])
    return both[:, :width] + both[:, width:] + dot(a_low, cat_ref[:, :width])


def chebyshev():
    stretch = CENTER / HALF_WIDTH
    rho = 1.0 / stretch
    out = []
    for _ in range(CHEB - 1):
        rho_next = 1.0 / (2.0 * stretch - rho)
        out.append((rho_next * rho, 2.0 * rho_next / HALF_WIDTH))
        rho = rho_next
    return out


def kernel(
    sizes,
    start_ref,
    len_ref,
    load_ref,
    first_ref,
    modes_ref,
    inverse_ref,
    mult_ref,
    operator_ref,
    dual_ref,
    final_ref,
    raw,
    op_high,
    op_low,
    product,
    load_t,
    lam,
    corr,
    res,
    weight,
    vec,
    modes_high,
    modes_low,
    modes_vec,
    modes_cat,
    image_cat,
    amp_cat,
    outgoing,
    landing,
    incoming,
    gathered,
    coeff,
    coeff_cat,
    inv_blocks,
    inv_high,
    inv_low,
    parts,
    arrived,
    places,
    raw_sem,
    halo_send,
    halo_recv,
    inv_send,
    inv_recv,
    coeff_send,
    coeff_recv,
    part_send,
    part_recv,
):
    nx, ny, nz = sizes
    m = product.shape[0] - PCAP
    loads = product.shape[1]
    nm = modes_ref.shape[0]
    tiles = m // TILE
    px, py, pz = (lax.axis_index(axis) for axis in AXES)
    spot = (px, py, pz)
    plane_me = py * nz + pz
    row_copies = m // PCAP

    plane = []
    for off in range(1, ny * nz):
        oy, oz = off // nz, off % nz
        plane.append({"gy": lax.rem(py + oy, ny), "gz": lax.rem(pz + oz, nz)})
    line = [lax.rem(px + off, nx) for off in range(1, nx)]

    barrier = pltpu.get_barrier_semaphore()
    for target in plane:
        pl.semaphore_signal(barrier, inc=1, device_id=target, device_id_type=MESH)
    for target in line:
        pl.semaphore_signal(barrier, inc=1, device_id={"gx": target}, device_id_type=MESH)

    def raw_copy(i):
        rows = pl.ds(i * PCAP, PCAP)
        return pltpu.make_async_copy(operator_ref.at[rows], raw.at[rows], raw_sem.at[i])

    for i in range(row_copies):
        raw_copy(i).start()

    lane = lax.broadcasted_iota(jnp.int32, (TILE, TILE), 1)
    for t in range(tiles):
        cols = slice(t * TILE, (t + 1) * TILE)
        load_t[cols, :] = load_ref[:, cols].T
        start_vec = first_ref[:, cols].T
        lam[cols, :] = start_vec
        high, low = split(start_vec)
        vec[cols, :loads] = high
        vec[cols, loads:] = low
        inverse_weight = 1.0 / mult_ref[:, cols].astype(F32)
        weight[cols, :] = jnp.broadcast_to(inverse_weight, (TILE, TILE)).T
        block = modes_ref[:, cols]
        high, low = split(block)
        modes_high[:, cols] = high
        modes_low[:, cols] = low
        twice = jnp.concatenate([block, block], axis=0).T
        high = twice.astype(BF16).astype(F32)
        low = twice - high
        modes_cat[cols, :TILE] = high.astype(BF16)
        modes_cat[cols, TILE:] = jnp.where(lane < nm, low, 0.0).astype(BF16)
        modes_vec[cols, :] = jnp.where(lane < nm, high, low).astype(BF16)
    corr[...] = jnp.zeros_like(corr)
    res[...] = jnp.zeros_like(res)
    incoming[...] = jnp.zeros_like(incoming)
    product[m:, :] = jnp.zeros((PCAP, loads), F32)

    for t in range(tiles):
        one = jnp.int32(0)
        two = jnp.int32(0)
        for f in range(6):
            rel = t * TILE - start_ref[f]
            hit = (rel > -TILE) & (rel < len_ref[f])
            at = TILE + SLOT * f + rel
            two = jnp.where(hit & (one > 0), at, two)
            one = jnp.where(hit & (one == 0), at, one)
        places[2 * t] = one
        places[2 * t + 1] = two

    pl.semaphore_wait(barrier, ny * nz - 1 + nx - 1)

    width = ny * nz * nm

    def inv_copy(i):
        cols = pl.ds(pl.multiple_of(line[i] * width, width), width)
        return pltpu.make_async_remote_copy(
            src_ref=inverse_ref.at[:, cols],
            dst_ref=inv_blocks.at[px],
            send_sem=inv_send.at[i],
            recv_sem=inv_recv.at[i],
            device_id={"gx": line[i]},
            device_id_type=MESH,
        )

    for i in range(nx - 1):
        inv_copy(i).start()
    inv_blocks[px] = inverse_ref[:, pl.ds(pl.multiple_of(px * width, width), width)]

    for i in range(row_copies):
        raw_copy(i).wait()

        @pl.loop(0, PCAP // 32)
        def _(k):
            rows = pl.ds(pl.multiple_of(i * PCAP + k * 32, 32), 32)
            high, low = split(raw[rows, :])
            op_high[rows, :] = high
            op_low[rows, :] = low

    def halo_copy(f, parity, arriving):
        dim, up = f // 2, f % 2
        near = spot[dim] + (1 if up else -1)
        slot = f if arriving else f ^ 1
        return pltpu.make_async_remote_copy(
            src_ref=outgoing.at[f],
            dst_ref=landing.at[parity, slot],
            send_sem=halo_send.at[f],
            recv_sem=halo_recv.at[parity, slot],
            device_id={AXES[dim]: near},
            device_id_type=MESH,
        )

    def has_near(f):
        dim, up = f // 2, f % 2
        return spot[dim] < sizes[dim] - 1 if up else spot[dim] > 0

    def coeff_copy(i, outer):
        return pltpu.make_async_remote_copy(
            src_ref=coeff,
            dst_ref=gathered.at[outer, plane_me],
            send_sem=coeff_send.at[i],
            recv_sem=coeff_recv.at[outer, i],
            device_id=plane[i],
            device_id_type=MESH,
        )

    def part_copy(i, outer):
        return pltpu.make_async_remote_copy(
            src_ref=parts.at[line[i]],
            dst_ref=arrived.at[outer, px],
            send_sem=part_send.at[i],
            recv_sem=part_recv.at[outer, i],
            device_id={"gx": line[i]},
            device_id_type=MESH,
        )

    coefs = chebyshev()
    steps = OUTER * CHEB
    row_in_piece = lax.broadcasted_iota(jnp.int32, (PCAP, loads), 0)

    @pl.loop(0, steps + 1)
    def _(n):
        stage = lax.rem(n, CHEB)
        parity = lax.rem(n, 2)

        @pl.loop(0, m // CHUNK)
        def _(k):
            rows = pl.ds(pl.multiple_of(k * CHUNK, CHUNK), CHUNK)
            product[rows, :] = triple(op_high[rows, :], op_low[rows, :], vec)

        @pl.when((stage == 0) & (n > 0))
        def _():
            outer = lax.div(n, CHEB) - 1

            @pl.when(outer == 0)
            def _():
                for i in range(nx - 1):
                    inv_copy(i).wait()
                for p in range(nx):
                    high, low = split(inv_blocks[p])
                    inv_high[p * nm : (p + 1) * nm, :] = high
                    inv_low[p * nm : (p + 1) * nm, :] = low

            for i in range(len(plane)):
                coeff_copy(i, outer).wait()
            for q in range(ny * nz):
                high, low = split(gathered[outer, q])
                coeff_cat[q * nm : (q + 1) * nm, :loads] = high
                coeff_cat[q * nm : (q + 1) * nm, loads:] = low
            part = triple(inv_high[...], inv_low[...], coeff_cat)
            for p in range(nx):
                parts[p] = part[p * nm : (p + 1) * nm, :]
            for i in range(nx - 1):
                part_copy(i, outer).start()
            arrived[outer, px] = parts[px]
            for i in range(nx - 1):
                part_copy(i, outer).wait()
            amp = arrived[outer, 0]
            for p in range(1, nx):
                amp = amp + arrived[outer, p]
            high, low = split(amp)
            amp_cat[0:nm, :] = high
            amp_cat[nm : 2 * nm, :] = low
            amp_cat[2 * nm : 3 * nm, :] = high
            amp_cat[3 * nm : 4 * nm, :] = jnp.zeros_like(high)
            product[0:m, :] = product[0:m, :] - dot(image_cat[...], amp_cat[...])

        for f in range(6):
            piece = product[pl.ds(start_ref[f], PCAP), :]
            outgoing[f] = jnp.where(row_in_piece < len_ref[f], piece, 0.0)

            @pl.when(has_near(f))
            def _():
                halo_copy(f, parity, False).start()

        @pl.when(n == 0)
        def _():
            @pl.loop(0, m // PCAP)
            def _(k):
                rows = pl.ds(pl.multiple_of(k * PCAP, PCAP), PCAP)
                one = dot(op_high[rows, :], modes_vec[...])
                two = dot(op_low[rows, :], modes_vec[...])
                left = lax.broadcasted_iota(jnp.int32, one.shape, 1) < nm
                image = one + pltpu.roll(one, nm, 1) + jnp.where(left, two, pltpu.roll(two, nm, 1))
                high = image.astype(BF16).astype(F32)
                image_cat[rows, :TILE] = high.astype(BF16)
                image_cat[rows, TILE:] = jnp.where(left, image - high, 0.0).astype(BF16)

        @pl.when((stage == 0) & (n > 0))
        def _():
            lam[...] = lam[...] - dot(modes_cat[...], amp_cat[...])

        for f in range(6):

            @pl.when(has_near(f))
            def _():
                halo_copy(f, parity, False).wait_send()
                halo_copy(f, parity, True).wait_recv()
                incoming[pl.ds(TILE + SLOT * f, PCAP), :] = landing[parity, f]

        keep = jnp.where(stage == 1, coefs[0][0], coefs[1][0]).astype(F32)
        keep = jnp.where(stage == 0, 0.0, keep)
        gain = jnp.where(stage == 1, coefs[0][1], coefs[1][1]).astype(F32)
        gain = jnp.where(stage == 0, 1.0, gain)
        add = jnp.where(n < steps, 1.0, 0.0).astype(F32)
        for t in range(tiles):
            rows = slice(t * TILE, (t + 1) * TILE)
            total = product[rows, :]
            total = total + incoming[pl.ds(places[2 * t], TILE), :]
            total = total + incoming[pl.ds(places[2 * t + 1], TILE), :]
            base = jnp.where(stage == 0, load_t[rows, :], res[rows, :])
            left_over = base - total * weight[rows, :]
            res[rows, :] = left_over
            step = keep * corr[rows, :] + gain * left_over
            corr[rows, :] = step
            grown = lam[rows, :] + add * step
            lam[rows, :] = grown
            high, low = split(jnp.where(stage == CHEB - 1, grown, step))
            vec[rows, :loads] = high
            vec[rows, loads:] = low

        @pl.when(stage == CHEB - 1)
        def _():
            outer = lax.div(n, CHEB)
            mine = triple(modes_high[...], modes_low[...], vec)
            coeff[...] = mine
            gathered[outer, plane_me] = mine
            for i in range(len(plane)):
                coeff_copy(i, outer).start()

    for t in range(tiles):
        cols = slice(t * TILE, (t + 1) * TILE)
        dual_ref[:, cols] = lam[cols, :].T
        final_ref[:, cols] = res[cols, :].T


def per_device(sizes, load, first, operator, modes, inverse, starts, lengths, mult):
    loads, m = load.shape[-2:]
    nm = modes.shape[-2]
    nx, ny, nz = sizes
    width = ny * nz * nm
    vmem = pl.BlockSpec(memory_space=pltpu.VMEM)
    smem = pl.BlockSpec(memory_space=pltpu.SMEM)
    dma = pltpu.SemaphoreType.DMA
    plane = max(ny * nz - 1, 1)
    line = max(nx - 1, 1)
    full = (m, loads)
    dual, final = pl.pallas_call(
        functools.partial(kernel, sizes),
        out_shape=[jax.ShapeDtypeStruct((loads, m), F32)] * 2,
        in_specs=[smem, smem] + [vmem] * 5 + [pl.BlockSpec(memory_space=pl.ANY)],
        out_specs=[vmem, vmem],
        scratch_shapes=[
            pltpu.VMEM((m, m), F32),
            pltpu.VMEM((m, m), BF16),
            pltpu.VMEM((m, m), BF16),
            pltpu.VMEM((m + PCAP, loads), F32),
            pltpu.VMEM(full, F32),
            pltpu.VMEM(full, F32),
            pltpu.VMEM(full, F32),
            pltpu.VMEM(full, F32),
            pltpu.VMEM(full, F32),
            pltpu.VMEM((m, 2 * loads), BF16),
            pltpu.VMEM((nm, m), BF16),
            pltpu.VMEM((nm, m), BF16),
            pltpu.VMEM((m, 2 * nm), BF16),
            pltpu.VMEM((m, 4 * nm), BF16),
            pltpu.VMEM((m, 4 * nm), BF16),
            pltpu.VMEM((4 * nm, loads), BF16),
            pltpu.VMEM((6, PCAP, loads), F32),
            pltpu.VMEM((2, 6, PCAP, loads), F32),
            pltpu.VMEM((6 * SLOT + TILE, loads), F32),
            pltpu.VMEM((OUTER, ny * nz, nm, loads), F32),
            pltpu.VMEM((nm, loads), F32),
            pltpu.VMEM((width, 2 * loads), BF16),
            pltpu.VMEM((nx, nm, width), F32),
            pltpu.VMEM((nx * nm, width), BF16),
            pltpu.VMEM((nx * nm, width), BF16),
            pltpu.VMEM((nx, nm, loads), F32),
            pltpu.VMEM((OUTER, nx, nm, loads), F32),
            pltpu.SMEM((2 * (m // TILE),), jnp.int32),
            dma((m // PCAP,)),
            dma((6,)),
            dma((2, 6)),
            dma((line,)),
            dma((line,)),
            dma((plane,)),
            dma((OUTER, plane)),
            dma((line,)),
            dma((OUTER, line)),
        ],
        compiler_params=pltpu.CompilerParams(
            collective_id=0, has_side_effects=True, vmem_limit_bytes=56 * 1024 * 1024
        ),
        cost_estimate=pl.CostEstimate(
            flops=2 * 3 * 7 * loads * m * m, bytes_accessed=4 * m * m, transcendentals=0
        ),
        name="feti_step",
    )(
        starts.reshape(-1),
        lengths.reshape(-1),
        load.reshape(loads, m),
        first.reshape(loads, m),
        modes.reshape(nm, m),
        inverse,
        mult.reshape(1, m),
        operator.reshape(m, m),
    )
    return dual.reshape(first.shape), final.reshape(first.shape)


def solution(mesh):
    block = P("gx", "gy", "gz", None, None)
    row = P("gx", "gy", "gz", None)
    sizes = tuple(mesh.shape[axis] for axis in AXES)
    return jax.shard_map(
        functools.partial(per_device, sizes),
        mesh=mesh,
        in_specs=(block, block, block, block, P(AXES, None), row, row, row),
        out_specs=(block, block),
        check_vma=False,
    )
```

```python
import functools

import jax
import jax.numpy as jnp
from jax import lax
from jax.experimental import pallas as pl
from jax.experimental.pallas import tpu as pltpu
from jax.sharding import PartitionSpec as P

PCAP = 256
OUTER = 2
CHEB = 3
TILE = 128
SLOT = PCAP + TILE
CHUNK = 768

CENTER = 1.0
HALF_WIDTH = 0.9

F32 = jnp.float32
BF16 = jnp.bfloat16
MESH = pl.DeviceIdType.MESH
AXES = ("gx", "gy", "gz")


def split(x):
    high = x.astype(BF16)
    return high, (x - high.astype(F32)).astype(BF16)


def dot(a, b):
    return jnp.dot(a, b, preferred_element_type=F32)


def triple(a_high, a_low, cat_ref):
    width = cat_ref.shape[1] // 2
    both = dot(a_high, cat_ref[...])
    return both[:, :width] + both[:, width:] + dot(a_low, cat_ref[:, :width])


def chebyshev():
    stretch = CENTER / HALF_WIDTH
    rho = 1.0 / stretch
    out = []
    for _ in range(CHEB - 1):
        rho_next = 1.0 / (2.0 * stretch - rho)
        out.append((rho_next * rho, 2.0 * rho_next / HALF_WIDTH))
        rho = rho_next
    return out


def kernel(
    sizes,
    start_ref,
    len_ref,
    load_ref,
    first_ref,
    modes_ref,
    inverse_ref,
    mult_ref,
    operator_ref,
    lam,
    res,
    raw,
    op_high,
    op_low,
    product,
    load_t,
    corr,
    weight,
    vec,
    modes_high,
    modes_low,
    modes_vec,
    modes_cat,
    image_cat,
    amp_cat,
    outgoing,
    landing,
    incoming,
    gathered,
    coeff,
    coeff_cat,
    inv_blocks,
    inv_high,
    inv_low,
    parts,
    arrived,
    places,
    raw_sem,
    halo_send,
    halo_recv,
    inv_send,
    inv_recv,
    coeff_send,
    coeff_recv,
    part_send,
    part_recv,
):
    nx, ny, nz = sizes
    m = product.shape[0] - PCAP
    loads = product.shape[1]
    nm = modes_ref.shape[0]
    tiles = m // TILE
    px, py, pz = (lax.axis_index(axis) for axis in AXES)
    spot = (px, py, pz)
    plane_me = px * nz + pz
    row_copies = m // PCAP

    plane = []
    for off in range(1, nx * nz):
        ox, oz = off // nz, off % nz
        plane.append({"gx": lax.rem(px + ox, nx), "gz": lax.rem(pz + oz, nz)})
    line = [lax.rem(py + off, ny) for off in range(1, ny)]

    barrier = pltpu.get_barrier_semaphore()
    for target in plane:
        pl.semaphore_signal(barrier, inc=1, device_id=target, device_id_type=MESH)
    for target in line:
        pl.semaphore_signal(barrier, inc=1, device_id={"gy": target}, device_id_type=MESH)

    def raw_copy(i):
        rows = pl.ds(i * PCAP, PCAP)
        return pltpu.make_async_copy(operator_ref.at[rows], raw.at[rows], raw_sem.at[i])

    for i in range(row_copies):
        raw_copy(i).start()

    lane = lax.broadcasted_iota(jnp.int32, (TILE, TILE), 1)
    for t in range(tiles):
        cols = slice(t * TILE, (t + 1) * TILE)
        load_t[cols, :] = load_ref[:, cols].T
        start_vec = first_ref[:, cols].T
        lam[cols, :] = start_vec
        high, low = split(start_vec)
        vec[cols, :loads] = high
        vec[cols, loads:] = low
        inverse_weight = 1.0 / mult_ref[:, cols].astype(F32)
        weight[cols, :] = jnp.broadcast_to(inverse_weight, (TILE, TILE)).T
        block = modes_ref[:, cols]
        high, low = split(block)
        modes_high[:, cols] = high
        modes_low[:, cols] = low
        twice = jnp.concatenate([block, block], axis=0).T
        high = twice.astype(BF16).astype(F32)
        low = twice - high
        modes_cat[cols, :TILE] = high.astype(BF16)
        modes_cat[cols, TILE:] = jnp.where(lane < nm, low, 0.0).astype(BF16)
        modes_vec[cols, :] = jnp.where(lane < nm, high, low).astype(BF16)
    corr[...] = jnp.zeros_like(corr)
    res[...] = jnp.zeros_like(res)
    incoming[...] = jnp.zeros_like(incoming)
    product[m:, :] = jnp.zeros((PCAP, loads), F32)

    for t in range(tiles):
        one = jnp.int32(0)
        two = jnp.int32(0)
        for f in range(6):
            rel = t * TILE - start_ref[f]
            hit = (rel > -TILE) & (rel < len_ref[f])
            at = TILE + SLOT * f + rel
            two = jnp.where(hit & (one > 0), at, two)
            one = jnp.where(hit & (one == 0), at, one)
        places[2 * t] = one
        places[2 * t + 1] = two

    pl.semaphore_wait(barrier, len(plane) + len(line))

    width = nz * nm

    def inv_columns(p, at):
        return pl.ds(pl.multiple_of((p * ny + at) * width, width), width)

    def inv_copy(i, p):
        return pltpu.make_async_remote_copy(
            src_ref=inverse_ref.at[:, inv_columns(p, line[i])],
            dst_ref=inv_blocks.at[py, p],
            send_sem=inv_send.at[i, p],
            recv_sem=inv_recv.at[i, p],
            device_id={"gy": line[i]},
            device_id_type=MESH,
        )

    for p in range(nx):
        for i in range(len(line)):
            inv_copy(i, p).start()
        inv_blocks[py, p] = inverse_ref[:, inv_columns(p, py)]

    for i in range(row_copies):
        raw_copy(i).wait()

        @pl.loop(0, PCAP // 32)
        def _(k):
            rows = pl.ds(pl.multiple_of(i * PCAP + k * 32, 32), 32)
            high, low = split(raw[rows, :])
            op_high[rows, :] = high
            op_low[rows, :] = low

    def halo_copy(f, parity, arriving):
        dim, up = f // 2, f % 2
        near = spot[dim] + (1 if up else -1)
        slot = f if arriving else f ^ 1
        return pltpu.make_async_remote_copy(
            src_ref=outgoing.at[f],
            dst_ref=landing.at[parity, slot],
            send_sem=halo_send.at[f],
            recv_sem=halo_recv.at[parity, slot],
            device_id={AXES[dim]: near},
            device_id_type=MESH,
        )

    def has_near(f):
        dim, up = f // 2, f % 2
        return spot[dim] < sizes[dim] - 1 if up else spot[dim] > 0

    def coeff_copy(i, outer):
        return pltpu.make_async_remote_copy(
            src_ref=coeff,
            dst_ref=gathered.at[outer, py],
            send_sem=coeff_send.at[i],
            recv_sem=coeff_recv.at[outer, i],
            device_id={"gy": line[i]},
            device_id_type=MESH,
        )

    def part_copy(i, outer):
        return pltpu.make_async_remote_copy(
            src_ref=parts.at[plane[i]["gx"] * nz + plane[i]["gz"]],
            dst_ref=arrived.at[outer, plane_me],
            send_sem=part_send.at[i],
            recv_sem=part_recv.at[outer, i],
            device_id=plane[i],
            device_id_type=MESH,
        )

    coefs = chebyshev()
    steps = OUTER * CHEB
    row_in_piece = lax.broadcasted_iota(jnp.int32, (PCAP, loads), 0)

    @pl.loop(0, steps + 1)
    def _(n):
        stage = lax.rem(n, CHEB)
        parity = lax.rem(n, 2)

        @pl.loop(0, m // CHUNK)
        def _(k):
            rows = pl.ds(pl.multiple_of(k * CHUNK, CHUNK), CHUNK)
            product[rows, :] = triple(op_high[rows, :], op_low[rows, :], vec)

        @pl.when((stage == 0) & (n > 0))
        def _():
            outer = lax.div(n, CHEB) - 1

            @pl.when(outer == 0)
            def _():
                for p in range(nx):
                    for i in range(len(line)):
                        inv_copy(i, p).wait()
                for p in range(nx):
                    for z in range(0, ny, 2):
                        pair = jnp.concatenate([inv_blocks[z, p], inv_blocks[z + 1, p]], axis=0)
                        high, low = split(pair.T)
                        inv_high[p * width : (p + 1) * width, z * nm : (z + 2) * nm] = high
                        inv_low[p * width : (p + 1) * width, z * nm : (z + 2) * nm] = low

            for i in range(len(line)):
                coeff_copy(i, outer).wait()
            for z in range(ny):
                high, low = split(gathered[outer, z])
                coeff_cat[z * nm : (z + 1) * nm, :loads] = high
                coeff_cat[z * nm : (z + 1) * nm, loads:] = low
            part = triple(inv_high[...], inv_low[...], coeff_cat)
            for p in range(nx * nz):
                parts[p] = part[p * nm : (p + 1) * nm, :]
            for i in range(len(plane)):
                part_copy(i, outer).start()
            arrived[outer, plane_me] = parts[plane_me]
            for i in range(len(plane)):
                part_copy(i, outer).wait()
            amp = arrived[outer, 0]
            for p in range(1, nx * nz):
                amp = amp + arrived[outer, p]
            high, low = split(amp)
            amp_cat[0:nm, :] = high
            amp_cat[nm : 2 * nm, :] = low
            amp_cat[2 * nm : 3 * nm, :] = high
            amp_cat[3 * nm : 4 * nm, :] = jnp.zeros_like(high)
            product[0:m, :] = product[0:m, :] - dot(image_cat[...], amp_cat[...])

        for f in range(6):
            piece = product[pl.ds(start_ref[f], PCAP), :]
            outgoing[f] = jnp.where(row_in_piece < len_ref[f], piece, 0.0)

            @pl.when(has_near(f))
            def _():
                halo_copy(f, parity, False).start()

        @pl.when(n == 0)
        def _():
            @pl.loop(0, m // PCAP)
            def _(k):
                rows = pl.ds(pl.multiple_of(k * PCAP, PCAP), PCAP)
                one = dot(op_high[rows, :], modes_vec[...])
                two = dot(op_low[rows, :], modes_vec[...])
                left = lax.broadcasted_iota(jnp.int32, one.shape, 1) < nm
                image = one + pltpu.roll(one, nm, 1) + jnp.where(left, two, pltpu.roll(two, nm, 1))
                high = image.astype(BF16).astype(F32)
                image_cat[rows, :TILE] = high.astype(BF16)
                image_cat[rows, TILE:] = jnp.where(left, image - high, 0.0).astype(BF16)

        @pl.when((stage == 0) & (n > 0))
        def _():
            lam[...] = lam[...] - dot(modes_cat[...], amp_cat[...])

        for f in range(6):

            @pl.when(has_near(f))
            def _():
                halo_copy(f, parity, False).wait_send()
                halo_copy(f, parity, True).wait_recv()
                incoming[pl.ds(TILE + SLOT * f, PCAP), :] = landing[parity, f]

        keep = jnp.where(stage == 1, coefs[0][0], coefs[1][0]).astype(F32)
        keep = jnp.where(stage == 0, 0.0, keep)
        gain = jnp.where(stage == 1, coefs[0][1], coefs[1][1]).astype(F32)
        gain = jnp.where(stage == 0, 1.0, gain)
        add = jnp.where(n < steps, 1.0, 0.0).astype(F32)
        for t in range(tiles):
            rows = slice(t * TILE, (t + 1) * TILE)
            total = product[rows, :]
            total = total + incoming[pl.ds(places[2 * t], TILE), :]
            total = total + incoming[pl.ds(places[2 * t + 1], TILE), :]
            base = jnp.where(stage == 0, load_t[rows, :], res[rows, :])
            left_over = base - total * weight[rows, :]
            res[rows, :] = left_over
            step = keep * corr[rows, :] + gain * left_over
            corr[rows, :] = step
            grown = lam[rows, :] + add * step
            lam[rows, :] = grown
            high, low = split(jnp.where(stage == CHEB - 1, grown, step))
            vec[rows, :loads] = high
            vec[rows, loads:] = low

        @pl.when(stage == CHEB - 1)
        def _():
            outer = lax.div(n, CHEB)
            mine = triple(modes_high[...], modes_low[...], vec)
            coeff[...] = mine
            gathered[outer, py] = mine
            for i in range(len(line)):
                coeff_copy(i, outer).start()


def turn(dual_t, final_t, dual_ref, final_ref):
    for k in range(0, dual_t.shape[0], TILE):
        cols = slice(k, k + TILE)
        dual_ref[:, cols] = dual_t[cols, :].T
        final_ref[:, cols] = final_t[cols, :].T


def per_device(sizes, load, first, operator, modes, inverse, starts, lengths, mult):
    loads, m = load.shape[-2:]
    nm = modes.shape[-2]
    nx, ny, nz = sizes
    width = nz * nm
    vmem = pl.BlockSpec(memory_space=pltpu.VMEM)
    smem = pl.BlockSpec(memory_space=pltpu.SMEM)
    dma = pltpu.SemaphoreType.DMA
    plane = nx * nz - 1
    line = ny - 1
    full = (m, loads)
    dual_t, final_t = pl.pallas_call(
        functools.partial(kernel, sizes),
        out_shape=[jax.ShapeDtypeStruct(full, F32)] * 2,
        in_specs=[smem, smem] + [vmem] * 5 + [pl.BlockSpec(memory_space=pl.ANY)],
        out_specs=[vmem, vmem],
        scratch_shapes=[
            pltpu.VMEM((m, m), F32),
            pltpu.VMEM((m, m), BF16),
            pltpu.VMEM((m, m), BF16),
            pltpu.VMEM((m + PCAP, loads), F32),
            pltpu.VMEM(full, F32),
            pltpu.VMEM(full, F32),
            pltpu.VMEM(full, F32),
            pltpu.VMEM((m, 2 * loads), BF16),
            pltpu.VMEM((nm, m), BF16),
            pltpu.VMEM((nm, m), BF16),
            pltpu.VMEM((m, 2 * nm), BF16),
            pltpu.VMEM((m, 4 * nm), BF16),
            pltpu.VMEM((m, 4 * nm), BF16),
            pltpu.VMEM((4 * nm, loads), BF16),
            pltpu.VMEM((6, PCAP, loads), F32),
            pltpu.VMEM((2, 6, PCAP, loads), F32),
            pltpu.VMEM((6 * SLOT + TILE, loads), F32),
            pltpu.VMEM((OUTER, ny, nm, loads), F32),
            pltpu.VMEM((nm, loads), F32),
            pltpu.VMEM((ny * nm, 2 * loads), BF16),
            pltpu.VMEM((ny, nx, nm, width), F32),
            pltpu.VMEM((nx * width, ny * nm), BF16),
            pltpu.VMEM((nx * width, ny * nm), BF16),
            pltpu.VMEM((nx * nz, nm, loads), F32),
            pltpu.VMEM((OUTER, nx * nz, nm, loads), F32),
            pltpu.SMEM((2 * (m // TILE),), jnp.int32),
            dma((m // PCAP,)),
            dma((6,)),
            dma((2, 6)),
            dma((line, nx)),
            dma((line, nx)),
            dma((line,)),
            dma((OUTER, line)),
            dma((plane,)),
            dma((OUTER, plane)),
        ],
        compiler_params=pltpu.CompilerParams(
            collective_id=0, has_side_effects=True, vmem_limit_bytes=56 * 1024 * 1024
        ),
        cost_estimate=pl.CostEstimate(
            flops=2 * 3 * 7 * loads * m * m, bytes_accessed=4 * m * m, transcendentals=0
        ),
        name="feti_step",
    )(
        starts.reshape(-1),
        lengths.reshape(-1),
        load.reshape(loads, m),
        first.reshape(loads, m),
        modes.reshape(nm, m),
        inverse,
        mult.reshape(1, m),
        operator.reshape(m, m),
    )
    step = m // 3 if m % (3 * TILE) == 0 else m
    rows = pl.BlockSpec((step, loads), lambda k: (k, 0))
    cols = pl.BlockSpec((loads, step), lambda k: (0, k))
    dual, final = pl.pallas_call(
        turn,
        grid=(m // step,),
        out_shape=[jax.ShapeDtypeStruct((loads, m), F32)] * 2,
        in_specs=[rows, rows],
        out_specs=[cols, cols],
        name="turn",
    )(dual_t, final_t)
    return dual.reshape(first.shape), final.reshape(first.shape)


def solution(mesh):
    block = P("gx", "gy", "gz", None, None)
    row = P("gx", "gy", "gz", None)
    sizes = tuple(mesh.shape[axis] for axis in AXES)
    return jax.shard_map(
        functools.partial(per_device, sizes),
        mesh=mesh,
        in_specs=(block, block, block, block, P(AXES, None), row, row, row),
        out_specs=(block, block),
        check_vma=False,
    )
```

```python
import functools

import jax
import jax.numpy as jnp
from jax import lax
from jax.experimental import pallas as pl
from jax.experimental.pallas import tpu as pltpu
from jax.sharding import PartitionSpec as P

PCAP = 256
OUTER = 2
CHEB = 3
TILE = 128
SLOT = PCAP + TILE
FACES = (2, 3, 4, 5, 0, 1)

CENTER = 1.0
HALF_WIDTH = 0.9

F32 = jnp.float32
BF16 = jnp.bfloat16
MESH = pl.DeviceIdType.MESH
AXES = ("gx", "gy", "gz")


def split(x):
    high = x.astype(BF16)
    return high, (x - high.astype(F32)).astype(BF16)


def dot(a, b):
    return jnp.dot(a, b, preferred_element_type=F32)


def triple(a_high, a_low, cat_ref):
    width = cat_ref.shape[1] // 2
    both = dot(a_high, cat_ref[...])
    return both[:, :width] + both[:, width:] + dot(a_low, cat_ref[:, :width])


def chebyshev():
    stretch = CENTER / HALF_WIDTH
    rho = 1.0 / stretch
    out = []
    for _ in range(CHEB - 1):
        rho_next = 1.0 / (2.0 * stretch - rho)
        out.append((rho_next * rho, 2.0 * rho_next / HALF_WIDTH))
        rho = rho_next
    return out


def kernel(
    sizes,
    start_ref,
    len_ref,
    load_ref,
    first_ref,
    modes_ref,
    inverse_ref,
    mult_ref,
    operator_ref,
    lam,
    res,
    raw,
    op_high,
    op_low,
    product,
    load_t,
    corr,
    weight,
    vec,
    modes_high,
    modes_low,
    modes_vec,
    modes_cat,
    image_cat,
    amp_cat,
    outgoing,
    landing,
    incoming,
    gathered,
    coeff,
    coeff_cat,
    inv_blocks,
    inv_high,
    inv_low,
    parts,
    arrived,
    places,
    raw_sem,
    halo_send,
    halo_recv,
    inv_send,
    inv_recv,
    coeff_send,
    coeff_recv,
    part_send,
    part_recv,
):
    nx, ny, nz = sizes
    m = product.shape[0] - PCAP
    loads = product.shape[1]
    nm = modes_ref.shape[0]
    tiles = m // TILE
    px, py, pz = (lax.axis_index(axis) for axis in AXES)
    spot = (px, py, pz)
    plane_me = py * nz + pz
    row_copies = m // PCAP

    plane = []
    for off in range(1, ny * nz):
        oy, oz = off // nz, off % nz
        plane.append({"gy": lax.rem(py + oy, ny), "gz": lax.rem(pz + oz, nz)})
    line = [lax.rem(px + off, nx) for off in range(1, nx)]

    barrier = pltpu.get_barrier_semaphore()
    for target in plane:
        pl.semaphore_signal(barrier, inc=1, device_id=target, device_id_type=MESH)
    for target in line:
        pl.semaphore_signal(barrier, inc=1, device_id={"gx": target}, device_id_type=MESH)

    def raw_copy(i):
        rows = pl.ds(i * PCAP, PCAP)
        return pltpu.make_async_copy(operator_ref.at[rows], raw.at[rows], raw_sem.at[i])

    for i in range(row_copies):
        raw_copy(i).start()

    lane = lax.broadcasted_iota(jnp.int32, (TILE, TILE), 1)
    for t in range(tiles):
        cols = slice(t * TILE, (t + 1) * TILE)
        load_t[cols, :] = load_ref[:, cols].T
        start_vec = first_ref[:, cols].T
        lam[cols, :] = start_vec
        high, low = split(start_vec)
        vec[cols, :loads] = high
        vec[cols, loads:] = low
        inverse_weight = 1.0 / mult_ref[:, cols].astype(F32)
        weight[cols, :] = jnp.broadcast_to(inverse_weight, (TILE, TILE)).T
        block = modes_ref[:, cols]
        high, low = split(block)
        modes_high[:, cols] = high
        modes_low[:, cols] = low
        twice = jnp.concatenate([block, block], axis=0).T
        high = twice.astype(BF16).astype(F32)
        low = twice - high
        modes_cat[cols, :TILE] = high.astype(BF16)
        modes_cat[cols, TILE:] = jnp.where(lane < nm, low, 0.0).astype(BF16)
        modes_vec[cols, :] = jnp.where(lane < nm, high, low).astype(BF16)
    corr[...] = jnp.zeros_like(corr)
    res[...] = jnp.zeros_like(res)
    incoming[...] = jnp.zeros_like(incoming)
    product[m:, :] = jnp.zeros((PCAP, loads), F32)

    for t in range(tiles):
        one = jnp.int32(0)
        two = jnp.int32(0)
        for f in range(6):
            rel = t * TILE - start_ref[f]
            hit = (rel > -TILE) & (rel < len_ref[f])
            at = TILE + SLOT * f + rel
            two = jnp.where(hit & (one > 0), at, two)
            one = jnp.where(hit & (one == 0), at, one)
        places[2 * t] = one
        places[2 * t + 1] = two

    pl.semaphore_wait(barrier, ny * nz - 1 + nx - 1)

    width = ny * nz * nm

    def inv_copy(i):
        cols = pl.ds(pl.multiple_of(line[i] * width, width), width)
        return pltpu.make_async_remote_copy(
            src_ref=inverse_ref.at[:, cols],
            dst_ref=inv_blocks.at[px],
            send_sem=inv_send.at[i],
            recv_sem=inv_recv.at[i],
            device_id={"gx": line[i]},
            device_id_type=MESH,
        )

    for i in range(nx - 1):
        inv_copy(i).start()
    inv_blocks[px] = inverse_ref[:, pl.ds(pl.multiple_of(px * width, width), width)]

    for i in range(row_copies):
        raw_copy(i).wait()

        @pl.loop(0, PCAP // 32)
        def _(k):
            rows = pl.ds(pl.multiple_of(i * PCAP + k * 32, 32), 32)
            high, low = split(raw[rows, :])
            op_high[rows, :] = high
            op_low[rows, :] = low

    def halo_copy(f, parity, arriving):
        dim, up = f // 2, f % 2
        near = spot[dim] + (1 if up else -1)
        slot = f if arriving else f ^ 1
        return pltpu.make_async_remote_copy(
            src_ref=outgoing.at[f],
            dst_ref=landing.at[parity, slot],
            send_sem=halo_send.at[f],
            recv_sem=halo_recv.at[parity, slot],
            device_id={AXES[dim]: near},
            device_id_type=MESH,
        )

    def has_near(f):
        dim, up = f // 2, f % 2
        return spot[dim] < sizes[dim] - 1 if up else spot[dim] > 0

    def coeff_copy(i, outer):
        return pltpu.make_async_remote_copy(
            src_ref=coeff,
            dst_ref=gathered.at[outer, plane_me],
            send_sem=coeff_send.at[i],
            recv_sem=coeff_recv.at[outer, i],
            device_id=plane[i],
            device_id_type=MESH,
        )

    def part_copy(i, outer):
        return pltpu.make_async_remote_copy(
            src_ref=parts.at[line[i]],
            dst_ref=arrived.at[outer, px],
            send_sem=part_send.at[i],
            recv_sem=part_recv.at[outer, i],
            device_id={"gx": line[i]},
            device_id_type=MESH,
        )

    coefs = chebyshev()
    steps = OUTER * CHEB
    row_in_piece = lax.broadcasted_iota(jnp.int32, (PCAP, loads), 0)

    @pl.loop(0, steps + 1)
    def _(n):
        stage = lax.rem(n, CHEB)
        parity = lax.rem(n, 2)

        product[0:m, :] = triple(op_high[...], op_low[...], vec)

        @pl.when((stage == 0) & (n > 0))
        def _():
            outer = lax.div(n, CHEB) - 1

            @pl.when(outer == 0)
            def _():
                for i in range(nx - 1):
                    inv_copy(i).wait()
                for p in range(nx):
                    high, low = split(inv_blocks[p])
                    inv_high[p * nm : (p + 1) * nm, :] = high
                    inv_low[p * nm : (p + 1) * nm, :] = low

            for i in range(len(plane)):
                coeff_copy(i, outer).wait()
            for q in range(ny * nz):
                high, low = split(gathered[outer, q])
                coeff_cat[q * nm : (q + 1) * nm, :loads] = high
                coeff_cat[q * nm : (q + 1) * nm, loads:] = low
            part = triple(inv_high[...], inv_low[...], coeff_cat)
            for p in range(nx):
                parts[p] = part[p * nm : (p + 1) * nm, :]
            for i in range(nx - 1):
                part_copy(i, outer).start()
            arrived[outer, px] = parts[px]
            for i in range(nx - 1):
                part_copy(i, outer).wait()
            amp = arrived[outer, 0]
            for p in range(1, nx):
                amp = amp + arrived[outer, p]
            high, low = split(amp)
            amp_cat[0:nm, :] = high
            amp_cat[nm : 2 * nm, :] = low
            amp_cat[2 * nm : 3 * nm, :] = high
            amp_cat[3 * nm : 4 * nm, :] = jnp.zeros_like(high)
            product[0:m, :] = product[0:m, :] - dot(image_cat[...], amp_cat[...])

        for f in FACES:
            piece = product[pl.ds(start_ref[f], PCAP), :]
            outgoing[f] = jnp.where(row_in_piece < len_ref[f], piece, 0.0)

            @pl.when(has_near(f))
            def _():
                halo_copy(f, parity, False).start()

        @pl.when(n == 0)
        def _():
            @pl.loop(0, m // PCAP)
            def _(k):
                rows = pl.ds(pl.multiple_of(k * PCAP, PCAP), PCAP)
                one = dot(op_high[rows, :], modes_vec[...])
                two = dot(op_low[rows, :], modes_vec[...])
                left = lax.broadcasted_iota(jnp.int32, one.shape, 1) < nm
                image = one + pltpu.roll(one, nm, 1) + jnp.where(left, two, pltpu.roll(two, nm, 1))
                high = image.astype(BF16).astype(F32)
                image_cat[rows, :TILE] = high.astype(BF16)
                image_cat[rows, TILE:] = jnp.where(left, image - high, 0.0).astype(BF16)

        @pl.when((stage == 0) & (n > 0))
        def _():
            lam[...] = lam[...] - dot(modes_cat[...], amp_cat[...])

        for t in range(tiles):
            rows = slice(t * TILE, (t + 1) * TILE)
            base = jnp.where(stage == 0, load_t[rows, :], res[rows, :])
            res[rows, :] = base - product[rows, :] * weight[rows, :]

        for f in reversed(FACES):

            @pl.when(has_near(f))
            def _():
                halo_copy(f, parity, False).wait_send()
                halo_copy(f, parity, True).wait_recv()
                incoming[pl.ds(TILE + SLOT * f, PCAP), :] = landing[parity, f]

        keep = jnp.where(stage == 1, coefs[0][0], coefs[1][0]).astype(F32)
        keep = jnp.where(stage == 0, 0.0, keep)
        gain = jnp.where(stage == 1, coefs[0][1], coefs[1][1]).astype(F32)
        gain = jnp.where(stage == 0, 1.0, gain)
        add = jnp.where(n < steps, 1.0, 0.0).astype(F32)
        for t in range(tiles):
            rows = slice(t * TILE, (t + 1) * TILE)
            halo = incoming[pl.ds(places[2 * t], TILE), :]
            halo = halo + incoming[pl.ds(places[2 * t + 1], TILE), :]
            left_over = res[rows, :] - halo * weight[rows, :]
            res[rows, :] = left_over
            step = keep * corr[rows, :] + gain * left_over
            corr[rows, :] = step
            grown = lam[rows, :] + add * step
            lam[rows, :] = grown
            high, low = split(jnp.where(stage == CHEB - 1, grown, step))
            vec[rows, :loads] = high
            vec[rows, loads:] = low

        @pl.when(stage == CHEB - 1)
        def _():
            outer = lax.div(n, CHEB)
            mine = triple(modes_high[...], modes_low[...], vec)
            coeff[...] = mine
            gathered[outer, plane_me] = mine
            for i in range(len(plane)):
                coeff_copy(i, outer).start()


def turn(dual_t, final_t, dual_ref, final_ref):
    for k in range(0, dual_t.shape[0], TILE):
        cols = slice(k, k + TILE)
        dual_ref[:, cols] = dual_t[cols, :].T
        final_ref[:, cols] = final_t[cols, :].T


def per_device(sizes, load, first, operator, modes, inverse, starts, lengths, mult):
    loads, m = load.shape[-2:]
    nm = modes.shape[-2]
    nx, ny, nz = sizes
    width = ny * nz * nm
    vmem = pl.BlockSpec(memory_space=pltpu.VMEM)
    smem = pl.BlockSpec(memory_space=pltpu.SMEM)
    dma = pltpu.SemaphoreType.DMA
    plane = max(ny * nz - 1, 1)
    line = max(nx - 1, 1)
    full = (m, loads)
    dual_t, final_t = pl.pallas_call(
        functools.partial(kernel, sizes),
        out_shape=[jax.ShapeDtypeStruct(full, F32)] * 2,
        in_specs=[smem, smem] + [vmem] * 5 + [pl.BlockSpec(memory_space=pl.ANY)],
        out_specs=[vmem, vmem],
        scratch_shapes=[
            pltpu.VMEM((m, m), F32),
            pltpu.VMEM((m, m), BF16),
            pltpu.VMEM((m, m), BF16),
            pltpu.VMEM((m + PCAP, loads), F32),
            pltpu.VMEM(full, F32),
            pltpu.VMEM(full, F32),
            pltpu.VMEM(full, F32),
            pltpu.VMEM((m, 2 * loads), BF16),
            pltpu.VMEM((nm, m), BF16),
            pltpu.VMEM((nm, m), BF16),
            pltpu.VMEM((m, 2 * nm), BF16),
            pltpu.VMEM((m, 4 * nm), BF16),
            pltpu.VMEM((m, 4 * nm), BF16),
            pltpu.VMEM((4 * nm, loads), BF16),
            pltpu.VMEM((6, PCAP, loads), F32),
            pltpu.VMEM((2, 6, PCAP, loads), F32),
            pltpu.VMEM((6 * SLOT + TILE, loads), F32),
            pltpu.VMEM((OUTER, ny * nz, nm, loads), F32),
            pltpu.VMEM((nm, loads), F32),
            pltpu.VMEM((width, 2 * loads), BF16),
            pltpu.VMEM((nx, nm, width), F32),
            pltpu.VMEM((nx * nm, width), BF16),
            pltpu.VMEM((nx * nm, width), BF16),
            pltpu.VMEM((nx, nm, loads), F32),
            pltpu.VMEM((OUTER, nx, nm, loads), F32),
            pltpu.SMEM((2 * (m // TILE),), jnp.int32),
            dma((m // PCAP,)),
            dma((6,)),
            dma((2, 6)),
            dma((line,)),
            dma((line,)),
            dma((plane,)),
            dma((OUTER, plane)),
            dma((line,)),
            dma((OUTER, line)),
        ],
        compiler_params=pltpu.CompilerParams(
            collective_id=0, has_side_effects=True, vmem_limit_bytes=56 * 1024 * 1024
        ),
        cost_estimate=pl.CostEstimate(
            flops=2 * 3 * 7 * loads * m * m, bytes_accessed=4 * m * m, transcendentals=0
        ),
        name="feti_step",
    )(
        starts.reshape(-1),
        lengths.reshape(-1),
        load.reshape(loads, m),
        first.reshape(loads, m),
        modes.reshape(nm, m),
        inverse,
        mult.reshape(1, m),
        operator.reshape(m, m),
    )
    dual, final = pl.pallas_call(
        turn,
        out_shape=[jax.ShapeDtypeStruct((loads, m), F32)] * 2,
        in_specs=[vmem, vmem],
        out_specs=[vmem, vmem],
        name="turn",
    )(dual_t, final_t)
    return dual.reshape(first.shape), final.reshape(first.shape)


def solution(mesh):
    block = P("gx", "gy", "gz", None, None)
    row = P("gx", "gy", "gz", None)
    sizes = tuple(mesh.shape[axis] for axis in AXES)
    return jax.shard_map(
        functools.partial(per_device, sizes),
        mesh=mesh,
        in_specs=(block, block, block, block, P(AXES, None), row, row, row),
        out_specs=(block, block),
        check_vma=False,
    )
```

```python
import functools

import jax
import jax.numpy as jnp
from jax import lax
from jax.experimental import pallas as pl
from jax.experimental.pallas import tpu as pltpu
from jax.sharding import PartitionSpec as P

PCAP = 256
OUTER = 2
CHEB = 3
TILE = 128
SLOT = PCAP + TILE
FACES = (2, 3, 4, 5, 0, 1)

CENTER = 1.0
HALF_WIDTH = 0.9

F32 = jnp.float32
BF16 = jnp.bfloat16
MESH = pl.DeviceIdType.MESH
AXES = ("gx", "gy", "gz")


def split(x):
    high = x.astype(BF16)
    return high, (x - high.astype(F32)).astype(BF16)


def dot(a, b):
    return jnp.dot(a, b, preferred_element_type=F32)


def triple(a_high, a_low, cat_ref):
    width = cat_ref.shape[1] // 2
    both = dot(a_high, cat_ref[...])
    return both[:, :width] + both[:, width:] + dot(a_low, cat_ref[:, :width])


def chebyshev():
    stretch = CENTER / HALF_WIDTH
    rho = 1.0 / stretch
    out = []
    for _ in range(CHEB - 1):
        rho_next = 1.0 / (2.0 * stretch - rho)
        out.append((rho_next * rho, 2.0 * rho_next / HALF_WIDTH))
        rho = rho_next
    return out


def kernel(
    sizes,
    start_ref,
    len_ref,
    load_any,
    first_any,
    modes_any,
    inverse_ref,
    mult_ref,
    operator_ref,
    res,
    dual_out,
    lam,
    raw,
    load_ref,
    first_ref,
    modes_ref,
    in_sem,
    own_sem,
    op_high,
    op_low,
    product,
    load_t,
    corr,
    weight,
    vec,
    modes_high,
    modes_low,
    modes_vec,
    modes_cat,
    image_cat,
    amp_cat,
    outgoing,
    landing,
    incoming,
    gathered,
    coeff,
    coeff_cat,
    inv_blocks,
    inv_high,
    inv_low,
    parts,
    arrived,
    places,
    raw_sem,
    halo_send,
    halo_recv,
    inv_send,
    inv_recv,
    coeff_send,
    coeff_recv,
    part_send,
    part_recv,
):
    nx, ny, nz = sizes
    m = product.shape[0] - PCAP
    loads = product.shape[1]
    nm = modes_ref.shape[0]
    tiles = m // TILE
    px, py, pz = (lax.axis_index(axis) for axis in AXES)
    spot = (px, py, pz)
    plane_me = py * nz + pz
    row_copies = m // PCAP

    plane = []
    for off in range(1, ny * nz):
        oy, oz = off // nz, off % nz
        plane.append({"gy": lax.rem(py + oy, ny), "gz": lax.rem(pz + oz, nz)})
    line = [lax.rem(px + off, nx) for off in range(1, nx)]

    pairs = ((modes_any, modes_ref), (first_any, first_ref), (load_any, load_ref))
    inputs = [pltpu.make_async_copy(a, b, in_sem.at[i]) for i, (a, b) in enumerate(pairs)]
    for copy in inputs:
        copy.start()

    barrier = pltpu.get_barrier_semaphore()
    for target in plane:
        pl.semaphore_signal(barrier, inc=1, device_id=target, device_id_type=MESH)
    for target in line:
        pl.semaphore_signal(barrier, inc=1, device_id={"gx": target}, device_id_type=MESH)

    def raw_copy(i):
        rows = pl.ds(i * PCAP, PCAP)
        return pltpu.make_async_copy(operator_ref.at[rows], raw.at[rows], raw_sem.at[i])

    for i in range(row_copies):
        raw_copy(i).start()

    lane = lax.broadcasted_iota(jnp.int32, (TILE, TILE), 1)
    for copy in inputs:
        copy.wait()
    for t in range(tiles):
        cols = slice(t * TILE, (t + 1) * TILE)
        load_t[cols, :] = load_ref[:, cols].T
        start_vec = first_ref[:, cols].T
        lam[cols, :] = start_vec
        high, low = split(start_vec)
        vec[cols, :loads] = high
        vec[cols, loads:] = low
        inverse_weight = 1.0 / mult_ref[:, cols].astype(F32)
        weight[cols, :] = jnp.broadcast_to(inverse_weight, (TILE, TILE)).T
        block = modes_ref[:, cols]
        high, low = split(block)
        modes_high[:, cols] = high
        modes_low[:, cols] = low
        twice = jnp.concatenate([block, block], axis=0).T
        high = twice.astype(BF16).astype(F32)
        low = twice - high
        modes_cat[cols, :TILE] = high.astype(BF16)
        modes_cat[cols, TILE:] = jnp.where(lane < nm, low, 0.0).astype(BF16)
        modes_vec[cols, :] = jnp.where(lane < nm, high, low).astype(BF16)
    corr[...] = jnp.zeros_like(corr)
    res[...] = jnp.zeros_like(res)
    incoming[...] = jnp.zeros_like(incoming)
    product[m:, :] = jnp.zeros((PCAP, loads), F32)

    for t in range(tiles):
        one = jnp.int32(0)
        two = jnp.int32(0)
        for f in range(6):
            rel = t * TILE - start_ref[f]
            hit = (rel > -TILE) & (rel < len_ref[f])
            at = TILE + SLOT * f + rel
            two = jnp.where(hit & (one > 0), at, two)
            one = jnp.where(hit & (one == 0), at, one)
        places[2 * t] = one
        places[2 * t + 1] = two

    pl.semaphore_wait(barrier, ny * nz - 1 + nx - 1)

    width = ny * nz * nm

    def inv_copy(i):
        cols = pl.ds(pl.multiple_of(line[i] * width, width), width)
        return pltpu.make_async_remote_copy(
            src_ref=inverse_ref.at[:, cols],
            dst_ref=inv_blocks.at[px],
            send_sem=inv_send.at[i],
            recv_sem=inv_recv.at[i],
            device_id={"gx": line[i]},
            device_id_type=MESH,
        )

    for i in range(nx - 1):
        inv_copy(i).start()
    own = pltpu.make_async_copy(
        inverse_ref.at[:, pl.ds(pl.multiple_of(px * width, width), width)],
        inv_blocks.at[px],
        own_sem,
    )
    own.start()

    for i in range(row_copies):
        raw_copy(i).wait()

        @pl.loop(0, PCAP // 32)
        def _(k):
            rows = pl.ds(pl.multiple_of(i * PCAP + k * 32, 32), 32)
            high, low = split(raw[rows, :])
            op_high[rows, :] = high
            op_low[rows, :] = low

    def halo_copy(f, parity, arriving):
        dim, up = f // 2, f % 2
        near = spot[dim] + (1 if up else -1)
        slot = f if arriving else f ^ 1
        return pltpu.make_async_remote_copy(
            src_ref=outgoing.at[f],
            dst_ref=landing.at[parity, slot],
            send_sem=halo_send.at[f],
            recv_sem=halo_recv.at[parity, slot],
            device_id={AXES[dim]: near},
            device_id_type=MESH,
        )

    def has_near(f):
        dim, up = f // 2, f % 2
        return spot[dim] < sizes[dim] - 1 if up else spot[dim] > 0

    def coeff_copy(i, outer):
        return pltpu.make_async_remote_copy(
            src_ref=coeff,
            dst_ref=gathered.at[outer, plane_me],
            send_sem=coeff_send.at[i],
            recv_sem=coeff_recv.at[outer, i],
            device_id=plane[i],
            device_id_type=MESH,
        )

    def part_copy(i, outer):
        return pltpu.make_async_remote_copy(
            src_ref=parts.at[line[i]],
            dst_ref=arrived.at[outer, px],
            send_sem=part_send.at[i],
            recv_sem=part_recv.at[outer, i],
            device_id={"gx": line[i]},
            device_id_type=MESH,
        )

    own.wait()
    coefs = chebyshev()
    steps = OUTER * CHEB
    row_in_piece = lax.broadcasted_iota(jnp.int32, (PCAP, loads), 0)

    @pl.loop(0, steps + 1)
    def _(n):
        stage = lax.rem(n, CHEB)
        parity = lax.rem(n, 2)

        outer = lax.div(n, CHEB) - 1
        half = m // 2
        product[0:half, :] = triple(op_high[0:half, :], op_low[0:half, :], vec)

        @pl.when((stage == 0) & (n > 0))
        def _():

            @pl.when(outer == 0)
            def _():
                for i in range(nx - 1):
                    inv_copy(i).wait()
                for p in range(nx):
                    high, low = split(inv_blocks[p])
                    inv_high[p * nm : (p + 1) * nm, :] = high
                    inv_low[p * nm : (p + 1) * nm, :] = low

            for i in range(len(plane)):
                coeff_copy(i, outer).wait()
            for q in range(ny * nz):
                high, low = split(gathered[outer, q])
                coeff_cat[q * nm : (q + 1) * nm, :loads] = high
                coeff_cat[q * nm : (q + 1) * nm, loads:] = low
            part = triple(inv_high[...], inv_low[...], coeff_cat)
            for p in range(nx):
                parts[p] = part[p * nm : (p + 1) * nm, :]
            for i in range(nx - 1):
                part_copy(i, outer).start()
            arrived[outer, px] = parts[px]

        product[half:m, :] = triple(op_high[half:m, :], op_low[half:m, :], vec)

        @pl.when((stage == 0) & (n > 0))
        def _():
            for i in range(nx - 1):
                part_copy(i, outer).wait()
            amp = arrived[outer, 0]
            for p in range(1, nx):
                amp = amp + arrived[outer, p]
            high, low = split(amp)
            amp_cat[0:nm, :] = high
            amp_cat[nm : 2 * nm, :] = low
            amp_cat[2 * nm : 3 * nm, :] = high
            amp_cat[3 * nm : 4 * nm, :] = jnp.zeros_like(high)
            product[0:m, :] = product[0:m, :] - dot(image_cat[...], amp_cat[...])

        for f in FACES:
            piece = product[pl.ds(start_ref[f], PCAP), :]
            outgoing[f] = jnp.where(row_in_piece < len_ref[f], piece, 0.0)

            @pl.when(has_near(f))
            def _():
                halo_copy(f, parity, False).start()

        @pl.when(n == 0)
        def _():
            @pl.loop(0, m // PCAP)
            def _(k):
                rows = pl.ds(pl.multiple_of(k * PCAP, PCAP), PCAP)
                one = dot(op_high[rows, :], modes_vec[...])
                two = dot(op_low[rows, :], modes_vec[...])
                left = lax.broadcasted_iota(jnp.int32, one.shape, 1) < nm
                image = one + pltpu.roll(one, nm, 1) + jnp.where(left, two, pltpu.roll(two, nm, 1))
                high = image.astype(BF16).astype(F32)
                image_cat[rows, :TILE] = high.astype(BF16)
                image_cat[rows, TILE:] = jnp.where(left, image - high, 0.0).astype(BF16)

        @pl.when((stage == 0) & (n > 0))
        def _():
            lam[...] = lam[...] - dot(modes_cat[...], amp_cat[...])

        @pl.when(n == steps)
        def _():
            for t in range(tiles):
                cols = slice(t * TILE, (t + 1) * TILE)
                dual_out[:, cols] = lam[cols, :].T

        for t in range(tiles):
            rows = slice(t * TILE, (t + 1) * TILE)
            base = jnp.where(stage == 0, load_t[rows, :], res[rows, :])
            res[rows, :] = base - product[rows, :] * weight[rows, :]

        for f in reversed(FACES):

            @pl.when(has_near(f))
            def _():
                halo_copy(f, parity, False).wait_send()
                halo_copy(f, parity, True).wait_recv()
                incoming[pl.ds(TILE + SLOT * f, PCAP), :] = landing[parity, f]

        keep = jnp.where(stage == 1, coefs[0][0], coefs[1][0]).astype(F32)
        keep = jnp.where(stage == 0, 0.0, keep)
        gain = jnp.where(stage == 1, coefs[0][1], coefs[1][1]).astype(F32)
        gain = jnp.where(stage == 0, 1.0, gain)
        add = jnp.where(n < steps, 1.0, 0.0).astype(F32)
        for t in range(tiles):
            rows = slice(t * TILE, (t + 1) * TILE)
            halo = incoming[pl.ds(places[2 * t], TILE), :]
            halo = halo + incoming[pl.ds(places[2 * t + 1], TILE), :]
            left_over = res[rows, :] - halo * weight[rows, :]
            res[rows, :] = left_over
            step = keep * corr[rows, :] + gain * left_over
            corr[rows, :] = step
            grown = lam[rows, :] + add * step
            lam[rows, :] = grown
            high, low = split(jnp.where(stage == CHEB - 1, grown, step))
            vec[rows, :loads] = high
            vec[rows, loads:] = low

        @pl.when(stage == CHEB - 1)
        def _():
            outer = lax.div(n, CHEB)
            mine = triple(modes_high[...], modes_low[...], vec)
            coeff[...] = mine
            gathered[outer, plane_me] = mine
            for i in range(len(plane)):
                coeff_copy(i, outer).start()


def turn(dual_in, final_t, dual_ref, final_ref):
    dual_ref[...] = dual_in[...]
    for k in range(0, final_t.shape[0], TILE):
        cols = slice(k, k + TILE)
        final_ref[:, cols] = final_t[cols, :].T


def per_device(sizes, load, first, operator, modes, inverse, starts, lengths, mult):
    loads, m = load.shape[-2:]
    nm = modes.shape[-2]
    nx, ny, nz = sizes
    width = ny * nz * nm
    vmem = pl.BlockSpec(memory_space=pltpu.VMEM)
    hbm = pl.BlockSpec(memory_space=pl.ANY)
    smem = pl.BlockSpec(memory_space=pltpu.SMEM)
    dma = pltpu.SemaphoreType.DMA
    plane = max(ny * nz - 1, 1)
    line = max(nx - 1, 1)
    full = (m, loads)
    final_t, dual_in = pl.pallas_call(
        functools.partial(kernel, sizes),
        out_shape=[jax.ShapeDtypeStruct(full, F32), jax.ShapeDtypeStruct((loads, m), F32)],
        in_specs=[smem, smem, hbm, hbm, hbm, hbm, vmem, hbm],
        out_specs=[vmem, vmem],
        scratch_shapes=[
            pltpu.VMEM(full, F32),
            pltpu.VMEM((m, m), F32),
            pltpu.VMEM((loads, m), F32),
            pltpu.VMEM((loads, m), F32),
            pltpu.VMEM((nm, m), F32),
            dma((3,)),
            dma,
            pltpu.VMEM((m, m), BF16),
            pltpu.VMEM((m, m), BF16),
            pltpu.VMEM((m + PCAP, loads), F32),
            pltpu.VMEM(full, F32),
            pltpu.VMEM(full, F32),
            pltpu.VMEM(full, F32),
            pltpu.VMEM((m, 2 * loads), BF16),
            pltpu.VMEM((nm, m), BF16),
            pltpu.VMEM((nm, m), BF16),
            pltpu.VMEM((m, 2 * nm), BF16),
            pltpu.VMEM((m, 4 * nm), BF16),
            pltpu.VMEM((m, 4 * nm), BF16),
            pltpu.VMEM((4 * nm, loads), BF16),
            pltpu.VMEM((6, PCAP, loads), F32),
            pltpu.VMEM((2, 6, PCAP, loads), F32),
            pltpu.VMEM((6 * SLOT + TILE, loads), F32),
            pltpu.VMEM((OUTER, ny * nz, nm, loads), F32),
            pltpu.VMEM((nm, loads), F32),
            pltpu.VMEM((width, 2 * loads), BF16),
            pltpu.VMEM((nx, nm, width), F32),
            pltpu.VMEM((nx * nm, width), BF16),
            pltpu.VMEM((nx * nm, width), BF16),
            pltpu.VMEM((nx, nm, loads), F32),
            pltpu.VMEM((OUTER, nx, nm, loads), F32),
            pltpu.SMEM((2 * (m // TILE),), jnp.int32),
            dma((m // PCAP,)),
            dma((6,)),
            dma((2, 6)),
            dma((line,)),
            dma((line,)),
            dma((plane,)),
            dma((OUTER, plane)),
            dma((line,)),
            dma((OUTER, line)),
        ],
        compiler_params=pltpu.CompilerParams(
            collective_id=0, has_side_effects=True, vmem_limit_bytes=56 * 1024 * 1024
        ),
        cost_estimate=pl.CostEstimate(
            flops=2 * 3 * 7 * loads * m * m, bytes_accessed=4 * m * m, transcendentals=0
        ),
        name="feti_step",
    )(
        starts.reshape(-1),
        lengths.reshape(-1),
        load.reshape(loads, m),
        first.reshape(loads, m),
        modes.reshape(nm, m),
        inverse,
        mult.reshape(1, m),
        operator.reshape(m, m),
    )
    dual, final = pl.pallas_call(
        turn,
        out_shape=[jax.ShapeDtypeStruct((loads, m), F32)] * 2,
        in_specs=[vmem, vmem],
        out_specs=[vmem, vmem],
        name="turn",
    )(dual_in, final_t)
    return dual.reshape(first.shape), final.reshape(first.shape)


def solution(mesh):
    block = P("gx", "gy", "gz", None, None)
    row = P("gx", "gy", "gz", None)
    sizes = tuple(mesh.shape[axis] for axis in AXES)
    return jax.shard_map(
        functools.partial(per_device, sizes),
        mesh=mesh,
        in_specs=(block, block, block, block, P(AXES, None), row, row, row),
        out_specs=(block, block),
        check_vma=False,
    )
```

```python
import functools

import jax
import jax.numpy as jnp
from jax import lax
from jax.experimental import pallas as pl
from jax.experimental.pallas import tpu as pltpu
from jax.sharding import PartitionSpec as P

PCAP = 256
OUTER = 2
CHEB = 3
TILE = 128
SLOT = PCAP + TILE
FACES = (2, 3, 4, 5, 0, 1)

CENTER = 1.0
HALF_WIDTH = 0.9

F32 = jnp.float32
BF16 = jnp.bfloat16
MESH = pl.DeviceIdType.MESH
AXES = ("gx", "gy", "gz")


def split(x):
    high = x.astype(BF16)
    return high, (x - high.astype(F32)).astype(BF16)


def dot(a, b):
    return jnp.dot(a, b, preferred_element_type=F32)


def triple(a_high, a_low, cat_ref):
    width = cat_ref.shape[1] // 2
    both = dot(a_high, cat_ref[...])
    return both[:, :width] + both[:, width:] + dot(a_low, cat_ref[:, :width])


def chebyshev():
    stretch = CENTER / HALF_WIDTH
    rho = 1.0 / stretch
    out = []
    for _ in range(CHEB - 1):
        rho_next = 1.0 / (2.0 * stretch - rho)
        out.append((rho_next * rho, 2.0 * rho_next / HALF_WIDTH))
        rho = rho_next
    return out


def kernel(
    sizes,
    start_ref,
    len_ref,
    load_any,
    first_any,
    modes_any,
    inverse_ref,
    mult_ref,
    operator_ref,
    res,
    dual_out,
    lam,
    raw,
    load_ref,
    first_ref,
    modes_ref,
    in_sem,
    own_sem,
    op_high,
    op_low,
    product,
    load_t,
    corr,
    weight,
    vec,
    modes_high,
    modes_low,
    modes_vec,
    modes_cat,
    image_cat,
    amp_cat,
    outgoing,
    landing,
    incoming,
    gathered,
    coeff,
    coeff_cat,
    inv_blocks,
    inv_high,
    inv_low,
    parts,
    arrived,
    places,
    raw_sem,
    halo_send,
    halo_recv,
    inv_send,
    inv_recv,
    coeff_send,
    coeff_recv,
    part_send,
    part_recv,
):
    nx, ny, nz = sizes
    m = product.shape[0] - PCAP
    loads = product.shape[1]
    nm = modes_ref.shape[0]
    tiles = m // TILE
    px, py, pz = (lax.axis_index(axis) for axis in AXES)
    spot = (px, py, pz)
    plane_me = py * nz + pz
    row_copies = m // PCAP

    plane = []
    for off in range(1, ny * nz):
        oy, oz = off // nz, off % nz
        plane.append({"gy": lax.rem(py + oy, ny), "gz": lax.rem(pz + oz, nz)})
    line = [lax.rem(px + off, nx) for off in range(1, nx)]

    pairs = ((modes_any, modes_ref), (first_any, first_ref), (load_any, load_ref))
    inputs = [pltpu.make_async_copy(a, b, in_sem.at[i]) for i, (a, b) in enumerate(pairs)]
    for copy in inputs:
        copy.start()

    barrier = pltpu.get_barrier_semaphore()
    for target in plane:
        pl.semaphore_signal(barrier, inc=1, device_id=target, device_id_type=MESH)
    for target in line:
        pl.semaphore_signal(barrier, inc=1, device_id={"gx": target}, device_id_type=MESH)

    def raw_copy(i):
        rows = pl.ds(i * PCAP, PCAP)
        return pltpu.make_async_copy(operator_ref.at[rows], raw.at[rows], raw_sem.at[i])

    for i in range(row_copies):
        raw_copy(i).start()

    lane = lax.broadcasted_iota(jnp.int32, (TILE, TILE), 1)
    for copy in inputs:
        copy.wait()
    for t in range(tiles):
        cols = slice(t * TILE, (t + 1) * TILE)
        load_t[cols, :] = load_ref[:, cols].T
        start_vec = first_ref[:, cols].T
        lam[cols, :] = start_vec
        high, low = split(start_vec)
        vec[cols, :loads] = high
        vec[cols, loads:] = low
        inverse_weight = 1.0 / mult_ref[:, cols].astype(F32)
        weight[cols, :] = jnp.broadcast_to(inverse_weight, (TILE, TILE)).T
        block = modes_ref[:, cols]
        high, low = split(block)
        modes_high[:, cols] = high
        modes_low[:, cols] = low
        twice = jnp.concatenate([block, block], axis=0).T
        high = twice.astype(BF16).astype(F32)
        low = twice - high
        modes_cat[cols, :TILE] = high.astype(BF16)
        modes_cat[cols, TILE:] = jnp.where(lane < nm, low, 0.0).astype(BF16)
        modes_vec[cols, :] = jnp.where(lane < nm, high, low).astype(BF16)
    corr[...] = jnp.zeros_like(corr)
    res[...] = jnp.zeros_like(res)
    incoming[...] = jnp.zeros_like(incoming)
    product[m:, :] = jnp.zeros((PCAP, loads), F32)

    for t in range(tiles):
        one = jnp.int32(0)
        two = jnp.int32(0)
        for f in range(6):
            rel = t * TILE - start_ref[f]
            hit = (rel > -TILE) & (rel < len_ref[f])
            at = TILE + SLOT * f + rel
            two = jnp.where(hit & (one > 0), at, two)
            one = jnp.where(hit & (one == 0), at, one)
        places[2 * t] = one
        places[2 * t + 1] = two

    pl.semaphore_wait(barrier, ny * nz - 1 + nx - 1)

    width = ny * nz * nm

    def inv_copy(i):
        cols = pl.ds(pl.multiple_of(line[i] * width, width), width)
        return pltpu.make_async_remote_copy(
            src_ref=inverse_ref.at[:, cols],
            dst_ref=inv_blocks.at[px],
            send_sem=inv_send.at[i],
            recv_sem=inv_recv.at[i],
            device_id={"gx": line[i]},
            device_id_type=MESH,
        )

    for i in range(nx - 1):
        inv_copy(i).start()
    own = pltpu.make_async_copy(
        inverse_ref.at[:, pl.ds(pl.multiple_of(px * width, width), width)],
        inv_blocks.at[px],
        own_sem,
    )
    own.start()

    for i in range(row_copies):
        raw_copy(i).wait()

        @pl.loop(0, PCAP // 32)
        def _(k):
            rows = pl.ds(pl.multiple_of(i * PCAP + k * 32, 32), 32)
            high, low = split(raw[rows, :])
            op_high[rows, :] = high
            op_low[rows, :] = low

    def halo_copy(f, parity, arriving):
        dim, up = f // 2, f % 2
        near = spot[dim] + (1 if up else -1)
        slot = f if arriving else f ^ 1
        return pltpu.make_async_remote_copy(
            src_ref=outgoing.at[f],
            dst_ref=landing.at[parity, slot],
            send_sem=halo_send.at[f],
            recv_sem=halo_recv.at[parity, slot],
            device_id={AXES[dim]: near},
            device_id_type=MESH,
        )

    def has_near(f):
        dim, up = f // 2, f % 2
        return spot[dim] < sizes[dim] - 1 if up else spot[dim] > 0

    def coeff_copy(i, outer):
        return pltpu.make_async_remote_copy(
            src_ref=coeff,
            dst_ref=gathered.at[outer, plane_me],
            send_sem=coeff_send.at[i],
            recv_sem=coeff_recv.at[outer, i],
            device_id=plane[i],
            device_id_type=MESH,
        )

    def part_copy(i, outer):
        return pltpu.make_async_remote_copy(
            src_ref=parts.at[line[i]],
            dst_ref=arrived.at[outer, px],
            send_sem=part_send.at[i],
            recv_sem=part_recv.at[outer, i],
            device_id={"gx": line[i]},
            device_id_type=MESH,
        )

    own.wait()
    coefs = chebyshev()
    steps = OUTER * CHEB
    row_in_piece = lax.broadcasted_iota(jnp.int32, (PCAP, loads), 0)

    @pl.loop(0, steps + 1)
    def _(n):
        stage = lax.rem(n, CHEB)
        parity = lax.rem(n, 2)

        outer = lax.div(n, CHEB) - 1
        product[0:m, :] = triple(op_high[...], op_low[...], vec)

        @pl.when((stage == 0) & (n > 0))
        def _():

            @pl.when(outer == 0)
            def _():
                for i in range(nx - 1):
                    inv_copy(i).wait()
                for p in range(nx):
                    high, low = split(inv_blocks[p])
                    inv_high[p * nm : (p + 1) * nm, :] = high
                    inv_low[p * nm : (p + 1) * nm, :] = low

            for i in range(len(plane)):
                coeff_copy(i, outer).wait()
            for q in range(ny * nz):
                high, low = split(gathered[outer, q])
                coeff_cat[q * nm : (q + 1) * nm, :loads] = high
                coeff_cat[q * nm : (q + 1) * nm, loads:] = low
            part = triple(inv_high[...], inv_low[...], coeff_cat)
            for p in range(nx):
                parts[p] = part[p * nm : (p + 1) * nm, :]
            for i in range(nx - 1):
                part_copy(i, outer).start()
            arrived[outer, px] = parts[px]
            for i in range(nx - 1):
                part_copy(i, outer).wait()
            amp = arrived[outer, 0]
            for p in range(1, nx):
                amp = amp + arrived[outer, p]
            high, low = split(amp)
            amp_cat[0:nm, :] = high
            amp_cat[nm : 2 * nm, :] = low
            amp_cat[2 * nm : 3 * nm, :] = high
            amp_cat[3 * nm : 4 * nm, :] = jnp.zeros_like(high)
            product[0:m, :] = product[0:m, :] - dot(image_cat[...], amp_cat[...])

        for f in FACES:
            piece = product[pl.ds(start_ref[f], PCAP), :]
            outgoing[f] = jnp.where(row_in_piece < len_ref[f], piece, 0.0)

            @pl.when(has_near(f))
            def _():
                halo_copy(f, parity, False).start()

        @pl.when(n == 0)
        def _():
            @pl.loop(0, m // PCAP)
            def _(k):
                rows = pl.ds(pl.multiple_of(k * PCAP, PCAP), PCAP)
                one = dot(op_high[rows, :], modes_vec[...])
                two = dot(op_low[rows, :], modes_vec[...])
                left = lax.broadcasted_iota(jnp.int32, one.shape, 1) < nm
                image = one + pltpu.roll(one, nm, 1) + jnp.where(left, two, pltpu.roll(two, nm, 1))
                high = image.astype(BF16).astype(F32)
                image_cat[rows, :TILE] = high.astype(BF16)
                image_cat[rows, TILE:] = jnp.where(left, image - high, 0.0).astype(BF16)

        @pl.when((stage == 0) & (n > 0))
        def _():
            lam[...] = lam[...] - dot(modes_cat[...], amp_cat[...])

        @pl.when(n == steps)
        def _():
            for t in range(tiles):
                cols = slice(t * TILE, (t + 1) * TILE)
                dual_out[:, cols] = lam[cols, :].T

        for t in range(tiles):
            rows = slice(t * TILE, (t + 1) * TILE)
            base = jnp.where(stage == 0, load_t[rows, :], res[rows, :])
            res[rows, :] = base - product[rows, :] * weight[rows, :]

        for f in reversed(FACES):

            @pl.when(has_near(f))
            def _():
                halo_copy(f, parity, False).wait_send()
                halo_copy(f, parity, True).wait_recv()
                incoming[pl.ds(TILE + SLOT * f, PCAP), :] = landing[parity, f]

        keep = jnp.where(stage == 1, coefs[0][0], coefs[1][0]).astype(F32)
        keep = jnp.where(stage == 0, 0.0, keep)
        gain = jnp.where(stage == 1, coefs[0][1], coefs[1][1]).astype(F32)
        gain = jnp.where(stage == 0, 1.0, gain)
        add = jnp.where(n < steps, 1.0, 0.0).astype(F32)
        for t in range(tiles):
            rows = slice(t * TILE, (t + 1) * TILE)
            halo = incoming[pl.ds(places[2 * t], TILE), :]
            halo = halo + incoming[pl.ds(places[2 * t + 1], TILE), :]
            left_over = res[rows, :] - halo * weight[rows, :]
            res[rows, :] = left_over
            step = keep * corr[rows, :] + gain * left_over
            corr[rows, :] = step
            grown = lam[rows, :] + add * step
            lam[rows, :] = grown
            high, low = split(jnp.where(stage == CHEB - 1, grown, step))
            vec[rows, :loads] = high
            vec[rows, loads:] = low

        @pl.when(stage == CHEB - 1)
        def _():
            outer = lax.div(n, CHEB)
            mine = triple(modes_high[...], modes_low[...], vec)
            coeff[...] = mine
            gathered[outer, plane_me] = mine
            for i in range(len(plane)):
                coeff_copy(i, outer).start()


def turn(dual_in, final_t, dual_ref, final_ref):
    dual_ref[...] = dual_in[...]
    for k in range(0, final_t.shape[0], TILE):
        cols = slice(k, k + TILE)
        final_ref[:, cols] = final_t[cols, :].T


def per_device(sizes, load, first, operator, modes, inverse, starts, lengths, mult):
    loads, m = load.shape[-2:]
    nm = modes.shape[-2]
    nx, ny, nz = sizes
    width = ny * nz * nm
    vmem = pl.BlockSpec(memory_space=pltpu.VMEM)
    hbm = pl.BlockSpec(memory_space=pl.ANY)
    smem = pl.BlockSpec(memory_space=pltpu.SMEM)
    dma = pltpu.SemaphoreType.DMA
    plane = max(ny * nz - 1, 1)
    line = max(nx - 1, 1)
    full = (m, loads)
    final_t, dual_in = pl.pallas_call(
        functools.partial(kernel, sizes),
        out_shape=[jax.ShapeDtypeStruct(full, F32), jax.ShapeDtypeStruct((loads, m), F32)],
        in_specs=[smem, smem, hbm, hbm, hbm, hbm, vmem, hbm],
        out_specs=[vmem, vmem],
        scratch_shapes=[
            pltpu.VMEM(full, F32),
            pltpu.VMEM((m, m), F32),
            pltpu.VMEM((loads, m), F32),
            pltpu.VMEM((loads, m), F32),
            pltpu.VMEM((nm, m), F32),
            dma((3,)),
            dma,
            pltpu.VMEM((m, m), BF16),
            pltpu.VMEM((m, m), BF16),
            pltpu.VMEM((m + PCAP, loads), F32),
            pltpu.VMEM(full, F32),
            pltpu.VMEM(full, F32),
            pltpu.VMEM(full, F32),
            pltpu.VMEM((m, 2 * loads), BF16),
            pltpu.VMEM((nm, m), BF16),
            pltpu.VMEM((nm, m), BF16),
            pltpu.VMEM((m, 2 * nm), BF16),
            pltpu.VMEM((m, 4 * nm), BF16),
            pltpu.VMEM((m, 4 * nm), BF16),
            pltpu.VMEM((4 * nm, loads), BF16),
            pltpu.VMEM((6, PCAP, loads), F32),
            pltpu.VMEM((2, 6, PCAP, loads), F32),
            pltpu.VMEM((6 * SLOT + TILE, loads), F32),
            pltpu.VMEM((OUTER, ny * nz, nm, loads), F32),
            pltpu.VMEM((nm, loads), F32),
            pltpu.VMEM((width, 2 * loads), BF16),
            pltpu.VMEM((nx, nm, width), F32),
            pltpu.VMEM((nx * nm, width), BF16),
            pltpu.VMEM((nx * nm, width), BF16),
            pltpu.VMEM((nx, nm, loads), F32),
            pltpu.VMEM((OUTER, nx, nm, loads), F32),
            pltpu.SMEM((2 * (m // TILE),), jnp.int32),
            dma((m // PCAP,)),
            dma((6,)),
            dma((2, 6)),
            dma((line,)),
            dma((line,)),
            dma((plane,)),
            dma((OUTER, plane)),
            dma((line,)),
            dma((OUTER, line)),
        ],
        compiler_params=pltpu.CompilerParams(
            collective_id=0, has_side_effects=True, vmem_limit_bytes=56 * 1024 * 1024
        ),
        cost_estimate=pl.CostEstimate(
            flops=2 * 3 * 7 * loads * m * m, bytes_accessed=4 * m * m, transcendentals=0
        ),
        name="feti_step",
    )(
        starts.reshape(-1),
        lengths.reshape(-1),
        load.reshape(loads, m),
        first.reshape(loads, m),
        modes.reshape(nm, m),
        inverse,
        mult.reshape(1, m),
        operator.reshape(m, m),
    )
    dual, final = pl.pallas_call(
        turn,
        out_shape=[jax.ShapeDtypeStruct((loads, m), F32)] * 2,
        in_specs=[vmem, vmem],
        out_specs=[vmem, vmem],
        name="turn",
    )(dual_in, final_t)
    return dual.reshape(first.shape), final.reshape(first.shape)


def solution(mesh):
    block = P("gx", "gy", "gz", None, None)
    row = P("gx", "gy", "gz", None)
    sizes = tuple(mesh.shape[axis] for axis in AXES)
    return jax.shard_map(
        functools.partial(per_device, sizes),
        mesh=mesh,
        in_specs=(block, block, block, block, P(AXES, None), row, row, row),
        out_specs=(block, block),
        check_vma=False,
    )
```
